32 devices in a mesh: tok: 8 (over z, x), feat: 4 (over y, core).
Axes of the slice: x: 2, y: 2, z: 4, core: 2. Of those that a mesh axis runs over, the one named last changes fastest.
Arguments:
- train_act: float32 [2048, 16384], P('tok', 'feat'), may hold values from -6 to 6
- train_grad: float32 [2048, 16384], P('tok', 'feat'), may hold values from -6 to 6
- pool_act: float32 [8, 16384], P('tok', 'feat'), may hold values from -6 to 6
- pool_grad: float32 [8, 16384], P('tok', 'feat'), may hold values from -6 to 6
- bite_index: int32 [4, 128], replicated, may hold values from 0 to 7, as said below
Outputs:
- score: float32 [2048], P(('tok', 'feat'))
The draws below stay inside these ranges and needn't reach their ends.
Inputs may be any that keep to these rules, and one draw needn't show every extreme that they name: `bite_index`: every pool token is named by at least one slot.
All inputs are finite; a program needn't handle non-finite values.
Results may differ from the reference program's by a relative error of at most 0.00017.
Values sent between devices are 32-bit elements; how exact they have to be, the bound alone decides.
No kernel may reach another device: no remote copies, remote signals or barrier semaphores. Data moves between devices by JAX's collectives and lax.ppermute only.
A program may use at most 64 MiB of HBM per device.

```python
import jax
import jax.numpy as jnp
from jax import lax

D = 16384
BITES = 4
BITE = 128
TRAIN = 2048
POOL = 8


def draw_bite_index(key, part):
    first_key = jax.random.fold_in(key, 11)
    second_key = jax.random.fold_in(key, 23)
    extra = jax.random.randint(first_key, (BITES * BITE - POOL,), 0, POOL, dtype=jnp.int32)
    every = jnp.concatenate([jnp.arange(POOL, dtype=jnp.int32), extra])
    mixed = jax.random.permutation(second_key, every)
    return mixed.reshape(BITES, BITE).astype(jnp.int32)


def shard_levels(own_key, dims, cuts, least, largest):
    factor_of, own = 1.0, jax.random.fold_in(own_key, 6)
    for position, blocks in cuts:
        draws = jnp.exp(jax.random.uniform(jax.random.fold_in(own, position), (blocks,), jnp.float32, least / len(cuts), largest / len(cuts)))
        factor_of = factor_of * jnp.repeat(draws, dims[position] // blocks).reshape([-1 if axis == position else 1 for axis in range(len(dims))])
    return factor_of


def scatter_about(key, extent, spread, most, split=(), kind=jnp.bfloat16):
    values = jax.random.normal(key, extent, jnp.float32) * spread
    if len(split) > 0:
        values = shard_levels(key, extent, split, -0.22, 0.18) * values
    return jnp.clip(values, min=-most, max=most).astype(kind)


def setup_inputs(seed: int = 0) -> dict:
    arg_keys = jax.random.split(jax.random.key(seed), 6)
    train_act = scatter_about(arg_keys[0], (TRAIN, D), 1.0, 6.0, ((0, 8), (1, 4)), jnp.float32)
    train_grad = scatter_about(arg_keys[1], (TRAIN, D), 1.0, 6.0, ((0, 8), (1, 4)), jnp.float32)
    pool_act = scatter_about(arg_keys[2], (POOL, D), 1.0, 6.0, ((0, 8), (1, 4)), jnp.float32)
    pool_grad = scatter_about(arg_keys[3], (POOL, D), 1.0, 6.0, ((0, 8), (1, 4)), jnp.float32)
    bite_index = draw_bite_index(jax.random.fold_in(arg_keys[5], 71), 0)
    return {"train_act": train_act, "train_grad": train_grad, "pool_act": pool_act, "pool_grad": pool_grad, "bite_index": bite_index}


def reference(train_act, train_grad, pool_act, pool_grad, bite_index):
    flat = bite_index.reshape(-1)
    pool_size = pool_act.shape[0]
    counts = lax.optimization_barrier(jnp.sum((flat[:, None] == jnp.arange(pool_size, dtype=jnp.int32)[None, :]).astype(jnp.float32), axis=0))
    act_gram = jnp.dot(train_act, pool_act.T, precision=lax.Precision.HIGHEST, preferred_element_type=jnp.float32)
    grad_gram = jnp.dot(train_grad, pool_grad.T, precision=lax.Precision.HIGHEST, preferred_element_type=jnp.float32)
    scale = 1.0 / (D * jnp.sqrt(jnp.float32(flat.shape[0])))
    return lax.optimization_barrier(jnp.sum(act_gram * grad_gram * counts[None, :], axis=1)) * scale
```

```python
import functools

import jax
import jax.numpy as jnp
from jax import lax
from jax.experimental import pallas as pl
from jax.experimental.pallas import tpu as pltpu
from jax.sharding import PartitionSpec as P

LANES = 128
CHUNKS = 8


def halves(x):
    hi = x.astype(jnp.bfloat16)
    lo = (x - hi.astype(jnp.float32)).astype(jnp.bfloat16)
    return hi, lo


def partner(index, step, size):
    if size & (size - 1) == 0:
        return index ^ step
    return (index + size - step) % size


def factors(n):
    outer = max(d for d in range(1, n + 1) if n % d == 0 and d * d <= n)
    return outer, n // outer


def vmem(*xs):
    return [pltpu.with_memory_space_constraint(x, pltpu.VMEM) for x in xs]


WHOLE = pl.BlockSpec(memory_space=pltpu.VMEM)
SMALL = pltpu.CompilerParams(vmem_limit_bytes=2 << 20)
ANYWHERE = pl.BlockSpec(memory_space=pl.ANY)


def prepare_kernel(act, grad, own, sems):
    block = act.shape[0]
    copies = [pltpu.make_async_copy(src, own.at[pl.ds(i * block, block)], sems.at[i]) for i, src in enumerate((act, grad))]
    for copy in copies:
        copy.start()
    for copy in copies:
        copy.wait()


def prepare(act, grad):
    return pl.pallas_call(
        prepare_kernel,
        out_shape=pltpu.VMEM((2 * act.shape[0], LANES), jnp.float32),
        in_specs=[ANYWHERE, ANYWHERE],
        out_specs=WHOLE,
        scratch_shapes=[pltpu.SemaphoreType.DMA((2,))],
        compiler_params=SMALL,
        name="prepare",
    )(pltpu.with_memory_space_constraint(act, pltpu.HBM), pltpu.with_memory_space_constraint(grad, pltpu.HBM))


def join_kernel(*refs):
    *parts, after, out = refs
    block = parts[0].shape[0]
    for i, part in enumerate(parts):
        out[pl.ds(i * block, block)] = part[...]


def join(parts, after):
    block = parts[0].shape[0]
    return pl.pallas_call(
        join_kernel,
        out_shape=pltpu.VMEM((len(parts) * block, LANES), jnp.float32),
        in_specs=[WHOLE] * len(parts) + [ANYWHERE],
        out_specs=WHOLE,
        compiler_params=SMALL,
        name="join",
    )(*vmem(*parts, after))


def weigh(outer, inner, width, bites, weight):
    n = outer * inner
    me = lax.axis_index("tok")
    row = lax.broadcasted_iota(jnp.int32, (n, LANES), 0)
    token = partner(me // inner, row % outer, outer) * inner + partner(me % inner, row // outer, inner)
    slots = bites.shape[0] * bites.shape[1]
    count = jnp.zeros((n, LANES), jnp.float32)
    for b in range(bites.shape[0]):
        for c in range(bites.shape[1] // LANES):
            count += (bites[b : b + 1, c * LANES : (c + 1) * LANES] == token).astype(jnp.float32)
    total = jnp.sum(count, axis=1, keepdims=True)
    weight[...] = jnp.broadcast_to(total * (1.0 / (width * slots**0.5)), (n, LANES))


def split_rows(train, hi, lo, buf, sems):
    step = train.shape[0] // CHUNKS
    copies = []
    for c in range(CHUNKS):
        copies.append(pltpu.make_async_copy(train.at[pl.ds(c * step, step)], buf.at[c], sems.at[c]))
        copies[c].start()
    for c in range(CHUNKS):
        copies[c].wait()

        @pl.loop(0, step // 16)
        def _(r):
            span = pl.ds(pl.multiple_of(r * 16, 16), 16)
            to = pl.ds(pl.multiple_of(c * step + r * 16, 16), 16)
            hi[to], lo[to] = halves(buf[c, span])


def split_act_kernel(outer, inner, width, train, bites, hi, lo, weight, buf, index, sems, sem):
    copy = pltpu.make_async_copy(bites, index, sem)
    copy.start()
    split_rows(train, hi, lo, buf, sems)
    copy.wait()
    weigh(outer, inner, width, index, weight)


def split_grad_kernel(train, after, hi, lo, buf, sems):
    split_rows(train, hi, lo, buf, sems)


def staging(train):
    return [pltpu.VMEM((CHUNKS, train.shape[0] // CHUNKS, train.shape[1]), jnp.float32)]


def hbm(*xs):
    return [pltpu.with_memory_space_constraint(x, pltpu.HBM) for x in xs]


def split_act(outer, inner, width, train, bites):
    half = pltpu.VMEM(train.shape, jnp.bfloat16)
    return pl.pallas_call(
        functools.partial(split_act_kernel, outer, inner, width),
        out_shape=[half, half, pltpu.VMEM((outer * inner, LANES), jnp.float32)],
        in_specs=[ANYWHERE] * 2,
        out_specs=[WHOLE] * 3,
        scratch_shapes=staging(train)
        + [pltpu.VMEM(bites.shape, jnp.int32), pltpu.SemaphoreType.DMA((CHUNKS,)), pltpu.SemaphoreType.DMA],
        compiler_params=pltpu.CompilerParams(vmem_limit_bytes=6 << 20),
        name="split_act",
    )(*hbm(train, bites))


def split_grad(train, after):
    half = pltpu.VMEM(train.shape, jnp.bfloat16)
    return pl.pallas_call(
        split_grad_kernel,
        out_shape=[half, half],
        in_specs=[ANYWHERE] * 2,
        out_specs=[WHOLE] * 2,
        scratch_shapes=staging(train) + [pltpu.SemaphoreType.DMA((CHUNKS,))],
        compiler_params=pltpu.CompilerParams(vmem_limit_bytes=6 << 20),
        name="split_grad",
    )(*hbm(train), *vmem(after))


def gram_kernel(outer, inner, feat, a_hi, a_lo, g_hi, g_lo, weight, *refs):
    pieces, (own, *sends), (pool,) = refs[:inner], refs[inner : inner + feat], refs[inner + feat :]
    n = outer * inner
    rows, cols = a_hi.shape
    block = pieces[0].shape[0] // outer
    for t in range(inner):
        pool[pl.ds(t * outer * block, outer * block)] = pieces[t][...]
    share = rows // feat
    results = []
    for which, hi, lo in ((0, a_hi, a_lo), (1, g_hi, g_lo)):
        tops, bottoms = [], []
        for q in range(cols // LANES):
            part = pool[pl.ds(which * (block // 2) + q, n, stride=block)]
            top, bottom = halves(part)
            tops.append(top)
            bottoms.append(bottom)
        p_hi = jnp.concatenate(tops, axis=1)
        p_lo = jnp.concatenate(bottoms, axis=1)
        both = jnp.concatenate([p_hi, p_lo], axis=0)
        dims = (((1,), (1,)), ((), ()))
        one = lax.dot_general(both, hi[...], dims, preferred_element_type=jnp.float32)
        two = lax.dot_general(p_hi, lo[...], dims, preferred_element_type=jnp.float32)
        results.append(one[:n] + one[n:] + two)
    act, grad = results
    act = act * jnp.tile(weight[...], (1, rows // LANES))
    me = lax.axis_index("feat")
    for j in range(feat):
        piece = jnp.concatenate([act[:, j * share : (j + 1) * share], grad[:, j * share : (j + 1) * share]], axis=1)
        for s, out in enumerate((own, *sends)):
            to = me ^ s if feat & (feat - 1) == 0 else (me + s) % feat

            @pl.when(to == j)
            def _():
                out[...] = piece


def grams(outer, inner, feat, parts, pieces):
    n = outer * inner
    rows, cols = parts[0].shape
    share = rows // feat
    args = vmem(*parts, *pieces)
    return pl.pallas_call(
        functools.partial(gram_kernel, outer, inner, feat),
        out_shape=[pltpu.VMEM((n, 2 * share), jnp.float32)] * feat,
        in_specs=[WHOLE] * len(args),
        out_specs=[WHOLE] * feat,
        scratch_shapes=[pltpu.VMEM((inner * pieces[0].shape[0], LANES), jnp.float32)],
        compiler_params=pltpu.CompilerParams(vmem_limit_bytes=8 << 20),
        name="grams",
    )(*args)


def finish_kernel(*refs):
    *parts, out = refs
    total = parts[0][...]
    for part in parts[1:]:
        total += part[...]
    share = out.shape[1]
    out[...] = jnp.sum(total[:, :share] * total[:, share:], axis=0, keepdims=True)


def body(train_act, train_grad, pool_act, pool_grad, bites):
    tok, feat = lax.axis_size("tok"), lax.axis_size("feat")
    rows, cols = train_act.shape
    outer, inner = factors(tok)
    own = prepare(pool_act.reshape(-1, LANES), pool_grad.reshape(-1, LANES))

    column = [own]
    for s in range(1, outer):
        pairs = [(partner(i // inner, s, outer) * inner + i % inner, i) for i in range(tok)]
        column.append(lax.ppermute(own, "tok", pairs))
    a_hi, a_lo, weight = split_act(outer, inner, cols * feat, train_act, bites)
    held = join(column, weight)
    pieces = [held]
    for t in range(1, inner):
        pairs = [(i // inner * inner + partner(i % inner, t, inner), i) for i in range(tok)]
        pieces.append(lax.ppermute(held, "tok", pairs))
    g_hi, g_lo = split_grad(train_grad, held)
    parts = a_hi, a_lo, g_hi, g_lo, weight
    mine, *sends = grams(outer, inner, feat, parts, pieces)
    got = [mine]
    for s, send in enumerate(sends, 1):
        pairs = [(i, i ^ s if feat & (feat - 1) == 0 else (i + s) % feat) for i in range(feat)]
        got.append(lax.ppermute(send, "feat", pairs))
    score = pl.pallas_call(
        finish_kernel,
        out_shape=jax.ShapeDtypeStruct((1, rows // feat), jnp.float32),
        in_specs=[WHOLE] * feat,
        out_specs=WHOLE,
        compiler_params=SMALL,
        name="finish",
    )(*vmem(*got))
    return score.reshape(-1)


def solution(mesh):
    return jax.shard_map(
        body,
        mesh=mesh,
        in_specs=(P("tok", "feat"), P("tok", "feat"), P("tok", "feat"), P("tok", "feat"), P()),
        out_specs=P(("tok", "feat")),
        check_vma=False,
    )
```

```python
import functools

import jax
import jax.numpy as jnp
from jax import lax
from jax.experimental import pallas as pl
from jax.experimental.pallas import tpu as pltpu
from jax.sharding import PartitionSpec as P

LANES = 128
CORES = 2


def halves(x):
    hi = x.astype(jnp.bfloat16)
    lo = (x - hi.astype(jnp.float32)).astype(jnp.bfloat16)
    return hi, lo


def partner(index, step, size):
    if size & (size - 1) == 0:
        return index ^ step
    return (index + size - step) % size


def partner_to(index, step, size):
    if size & (size - 1) == 0:
        return index ^ step
    return (index + step) % size


def factors(n):
    outer = max(d for d in range(1, n + 1) if n % d == 0 and d * d <= n)
    return outer, n // outer


def vmem(*xs):
    return [pltpu.with_memory_space_constraint(x, pltpu.VMEM) for x in xs]


WHOLE = pl.BlockSpec(memory_space=pltpu.VMEM)
SMALL = pltpu.CompilerParams(vmem_limit_bytes=2 << 20)
ANYWHERE = pl.BlockSpec(memory_space=pl.ANY)


def prepare_kernel(act, grad, own, sems):
    block = act.shape[0]
    copies = [pltpu.make_async_copy(src, own.at[pl.ds(i * block, block)], sems.at[i]) for i, src in enumerate((act, grad))]
    for copy in copies:
        copy.start()
    for copy in copies:
        copy.wait()


def prepare(act, grad):
    return pl.pallas_call(
        prepare_kernel,
        out_shape=pltpu.VMEM((2 * act.shape[0], LANES), jnp.float32),
        in_specs=[ANYWHERE, ANYWHERE],
        out_specs=WHOLE,
        scratch_shapes=[pltpu.SemaphoreType.DMA((2,))],
        compiler_params=SMALL,
        name="prepare",
    )(pltpu.with_memory_space_constraint(act, pltpu.HBM), pltpu.with_memory_space_constraint(grad, pltpu.HBM))


def stage_kernel(own, train_act, train_grad, out):
    out[...] = own[...]


def stage(own, *trains):
    return pl.pallas_call(
        stage_kernel,
        out_shape=pltpu.VMEM(own.shape, jnp.float32),
        in_specs=[WHOLE, ANYWHERE, ANYWHERE],
        out_specs=WHOLE,
        compiler_params=SMALL,
        name="stage",
    )(*vmem(own), *[pltpu.with_memory_space_constraint(x, pltpu.HBM) for x in trains])


def join_kernel(*refs):
    *parts, out = refs
    block = parts[0].shape[0]
    for i, part in enumerate(parts):
        out[pl.ds(i * block, block)] = part[...]


def join(parts):
    block = parts[0].shape[0]
    return pl.pallas_call(
        join_kernel,
        out_shape=pltpu.VMEM((len(parts) * block, LANES), jnp.float32),
        in_specs=[WHOLE] * len(parts),
        out_specs=WHOLE,
        compiler_params=SMALL,
        name="join",
    )(*vmem(*parts))


def weigh(outer, inner, width, bites, weight):
    n = outer * inner
    me = lax.axis_index("tok")
    row = lax.broadcasted_iota(jnp.int32, (n, LANES), 0)
    token = partner(me // inner, row % outer, outer) * inner + partner(me % inner, row // outer, inner)
    slots = bites.shape[0] * bites.shape[1]
    count = jnp.zeros((n, LANES), jnp.float32)
    for b in range(bites.shape[0]):
        for c in range(bites.shape[1] // LANES):
            count += (bites[b : b + 1, c * LANES : (c + 1) * LANES] == token).astype(jnp.float32)
    total = jnp.sum(count, axis=1, keepdims=True)
    weight[...] = jnp.broadcast_to(total * (1.0 / (width * slots**0.5)), (n, LANES))


def split_rows(train, hi, lo):
    @pl.loop(0, train.shape[0] // 16)
    def _(r):
        span = pl.ds(pl.multiple_of(r * 16, 16), 16)
        hi[span], lo[span] = halves(train[span])


def split_kernel(outer, inner, width, act, grad, bites, after, a_hi, a_lo, g_hi, g_lo, weight, index, sem):
    copy = pltpu.make_async_copy(bites, index, sem)
    copy.start()
    split_rows(act, a_hi, a_lo)
    split_rows(grad, g_hi, g_lo)
    copy.wait()
    weigh(outer, inner, width, index, weight)


def split(outer, inner, width, act, grad, bites, after):
    half = pltpu.VMEM(act.shape, jnp.bfloat16)
    return pl.pallas_call(
        functools.partial(split_kernel, outer, inner, width),
        out_shape=[half] * 4 + [pltpu.VMEM((outer * inner, LANES), jnp.float32)],
        in_specs=[WHOLE, WHOLE, ANYWHERE, ANYWHERE],
        out_specs=[WHOLE] * 5,
        scratch_shapes=[pltpu.VMEM(bites.shape, jnp.int32), pltpu.SemaphoreType.DMA],
        compiler_params=SMALL,
        name="split",
    )(*vmem(act, grad), pltpu.with_memory_space_constraint(bites, pltpu.HBM), *vmem(after))


def rows_of(pool, which, n, cols, block):
    tops, bottoms = [], []
    for q in range(cols // LANES):
        top, bottom = halves(pool[pl.ds(which * (block // 2) + q, n, stride=block)])
        tops.append(top)
        bottoms.append(bottom)
    return jnp.concatenate([jnp.concatenate(tops, axis=1), jnp.concatenate(bottoms, axis=1)], axis=0)


def product(both, hi, lo, start, rows):
    n = both.shape[0] // 2
    dims = (((1,), (1,)), ((), ()))
    span = pl.ds(pl.multiple_of(start, 32), rows)
    one = lax.dot_general(both, hi[span], dims, preferred_element_type=jnp.float32)
    two = lax.dot_general(both[:n], lo[span], dims, preferred_element_type=jnp.float32)
    return one[:n] + one[n:] + two


def device_grams(act_pool, grad_pool, parts, weight, to, share):
    a_hi, a_lo, g_hi, g_lo = parts
    act = product(act_pool[...], a_hi, a_lo, to * share, share) * weight[:, :share]
    grad = product(grad_pool[...], g_hi, g_lo, to * share, share)
    return jnp.concatenate([act, grad], axis=1)


def chip_grams(act_pool, grad_pool, parts, weight, chip, share):
    a_hi, a_lo, g_hi, g_lo = parts
    rows = CORES * share
    act = product(act_pool[...], a_hi, a_lo, chip * rows, rows) * weight[:, :rows]
    grad = product(grad_pool[...], g_hi, g_lo, chip * rows, rows)
    return [
        jnp.concatenate([act[:, c * share : (c + 1) * share], grad[:, c * share : (c + 1) * share]], axis=1)
        for c in range(CORES)
    ]


def swap(pieces, me, mine, other):
    mine[...] = jnp.where(me % CORES == 0, pieces[0], pieces[1])
    other[...] = jnp.where(me % CORES == 0, pieces[1], pieces[0])


def far_kernel(outer, inner, feat, a_hi, a_lo, g_hi, g_lo, weight, *refs):
    pieces, (act_pool, grad_pool, *outs), (pool,) = refs[:inner], refs[inner:-1], refs[-1:]
    n = outer * inner
    rows, cols = a_hi.shape
    block = pieces[0].shape[0] // outer
    start = 0
    for piece in pieces:
        pool[pl.ds(start, piece.shape[0])] = piece[...]
        start += piece.shape[0]
    act_pool[...] = rows_of(pool, 0, n, cols, block)
    grad_pool[...] = rows_of(pool, 1, n, cols, block)
    me = lax.axis_index("feat")
    chips = feat // CORES
    for s in range(1, chips):
        to = partner_to(me // CORES, s, chips)
        got = chip_grams(act_pool, grad_pool, (a_hi, a_lo, g_hi, g_lo), weight, to, rows // feat)
        swap(got, me, outs[CORES * (s - 1)], outs[CORES * (s - 1) + 1])


def near_kernel(feat, step, a_hi, a_lo, g_hi, g_lo, weight, act_pool, grad_pool, after, out):
    me = lax.axis_index("feat")
    to = me // CORES * CORES + (me + step) % CORES
    out[...] = device_grams(act_pool, grad_pool, (a_hi, a_lo, g_hi, g_lo), weight, to, a_hi.shape[0] // feat)


def far(outer, inner, feat, parts, pieces):
    n = outer * inner
    rows, cols = parts[0].shape
    args = vmem(*parts, *pieces)
    piece = pltpu.VMEM((n, 2 * rows // feat), jnp.float32)
    outs = [pltpu.VMEM((2 * n, cols), jnp.bfloat16)] * 2 + [piece] * (feat - CORES)
    return pl.pallas_call(
        functools.partial(far_kernel, outer, inner, feat),
        out_shape=outs,
        in_specs=[WHOLE] * len(args),
        out_specs=[WHOLE] * len(outs),
        scratch_shapes=[pltpu.VMEM((inner * pieces[0].shape[0], LANES), jnp.float32)],
        compiler_params=pltpu.CompilerParams(vmem_limit_bytes=8 << 20),
        name="far",
    )(*args)


def near(feat, step, parts, pools, after):
    args = vmem(*parts, *pools, after)
    return pl.pallas_call(
        functools.partial(near_kernel, feat, step),
        out_shape=pltpu.VMEM((pools[0].shape[0] // 2, 2 * parts[0].shape[0] // feat), jnp.float32),
        in_specs=[WHOLE] * (len(args) - 1) + [ANYWHERE],
        out_specs=WHOLE,
        compiler_params=pltpu.CompilerParams(vmem_limit_bytes=8 << 20),
        name="near",
    )(*args)


def add_kernel(*refs):
    *parts, out = refs
    total = parts[0][...]
    for part in parts[1:]:
        total += part[...]
    out[...] = total


def tally(parts):
    return pl.pallas_call(
        add_kernel,
        out_shape=pltpu.VMEM(parts[0].shape, jnp.float32),
        in_specs=[WHOLE] * len(parts),
        out_specs=WHOLE,
        compiler_params=SMALL,
        name="add",
    )(*vmem(*parts))


def finish_kernel(*refs):
    *parts, out = refs
    total = parts[0][...]
    for part in parts[1:]:
        total += part[...]
    share = out.shape[1]
    out[...] = jnp.sum(total[:, :share] * total[:, share:], axis=0, keepdims=True)


def body(train_act, train_grad, pool_act, pool_grad, bites):
    tok, feat = lax.axis_size("tok"), lax.axis_size("feat")
    rows, cols = train_act.shape
    outer, inner = factors(tok)
    own = prepare(pool_act.reshape(-1, LANES), pool_grad.reshape(-1, LANES))

    own = stage(own, train_act, train_grad)
    across = [[(partner(i // inner, s, outer) * inner + i % inner, i) for i in range(tok)] for s in range(1, outer)]
    along = [[(i // inner * inner + partner(i % inner, t, inner), i) for i in range(tok)] for t in range(1, inner)]
    held = join([own] + [lax.ppermute(own, "tok", pairs) for pairs in across])
    pieces = [held] + [lax.ppermute(held, "tok", pairs) for pairs in along]
    parts = split(outer, inner, cols * feat, train_act, train_grad, bites, held)
    act_pool, grad_pool, *sends = far(outer, inner, feat, parts, pieces)
    chips = feat // CORES
    got = []
    for s, send in enumerate(sends, CORES):
        pairs = [(i, partner_to(i // CORES, s // CORES, chips) * CORES + (i + s) % CORES) for i in range(feat)]
        got.append(lax.ppermute(send, "feat", pairs))
    other = near(feat, 1, parts, (act_pool, grad_pool), sends[0])
    beside = lax.ppermute(other, "feat", [(i, i // CORES * CORES + (i + 1) % CORES) for i in range(feat)])
    got = [tally([*got, near(feat, 0, parts, (act_pool, grad_pool), other)]), beside]
    score = pl.pallas_call(
        finish_kernel,
        out_shape=jax.ShapeDtypeStruct((1, rows // feat), jnp.float32),
        in_specs=[WHOLE] * len(got),
        out_specs=WHOLE,
        compiler_params=SMALL,
        name="finish",
    )(*vmem(*got))
    return score.reshape(-1)


def solution(mesh):
    return jax.shard_map(
        body,
        mesh=mesh,
        in_specs=(P("tok", "feat"), P("tok", "feat"), P("tok", "feat"), P("tok", "feat"), P()),
        out_specs=P(("tok", "feat")),
        check_vma=False,
    )
```

```python
import functools

import jax
import jax.numpy as jnp
from jax import lax
from jax.experimental import pallas as pl
from jax.experimental.pallas import tpu as pltpu
from jax.sharding import PartitionSpec as P

LANES = 128
CORES = 2


def halves(x):
    hi = x.astype(jnp.bfloat16)
    lo = (x - hi.astype(jnp.float32)).astype(jnp.bfloat16)
    return hi, lo


def partner(index, step, size):
    if size & (size - 1) == 0:
        return index ^ step
    return (index + size - step) % size


def partner_to(index, step, size):
    if size & (size - 1) == 0:
        return index ^ step
    return (index + step) % size


def factors(n):
    outer = max(d for d in range(1, n + 1) if n % d == 0 and d * d <= n)
    return outer, n // outer


def order(inner):
    apart = inner // 2
    return [t for t in range(1, inner) if t != apart] + [apart]


def vmem(*xs):
    return [pltpu.with_memory_space_constraint(x, pltpu.VMEM) for x in xs]


WHOLE = pl.BlockSpec(memory_space=pltpu.VMEM)
SMALL = pltpu.CompilerParams(vmem_limit_bytes=2 << 20)
ANYWHERE = pl.BlockSpec(memory_space=pl.ANY)


def prepare_kernel(act, grad, own, sems):
    block = act.shape[0]
    copies = [pltpu.make_async_copy(src, own.at[pl.ds(i * block, block)], sems.at[i]) for i, src in enumerate((act, grad))]
    for copy in copies:
        copy.start()
    for copy in copies:
        copy.wait()


def prepare(act, grad):
    return pl.pallas_call(
        prepare_kernel,
        out_shape=pltpu.VMEM((2 * act.shape[0], LANES), jnp.float32),
        in_specs=[ANYWHERE, ANYWHERE],
        out_specs=WHOLE,
        scratch_shapes=[pltpu.SemaphoreType.DMA((2,))],
        compiler_params=SMALL,
        name="prepare",
    )(pltpu.with_memory_space_constraint(act, pltpu.HBM), pltpu.with_memory_space_constraint(grad, pltpu.HBM))


def stage_kernel(own, train_act, train_grad, out):
    out[...] = own[...]


def stage(own, *trains):
    return pl.pallas_call(
        stage_kernel,
        out_shape=pltpu.VMEM(own.shape, jnp.float32),
        in_specs=[WHOLE, ANYWHERE, ANYWHERE],
        out_specs=WHOLE,
        compiler_params=SMALL,
        name="stage",
    )(*vmem(own), *[pltpu.with_memory_space_constraint(x, pltpu.HBM) for x in trains])


def join_kernel(count, *refs):
    out = refs[-1]
    block = refs[0].shape[0]
    for i, part in enumerate(refs[:count]):
        out[pl.ds(i * block, block)] = part[...]


def join(parts, *after):
    block = parts[0].shape[0]
    return pl.pallas_call(
        functools.partial(join_kernel, len(parts)),
        out_shape=pltpu.VMEM((len(parts) * block, LANES), jnp.float32),
        in_specs=[WHOLE] * len(parts) + [ANYWHERE] * len(after),
        out_specs=WHOLE,
        compiler_params=SMALL,
        name="join",
    )(*vmem(*parts, *after))


def weigh(outer, inner, width, bites, weight):
    n = outer * inner
    me = lax.axis_index("tok")
    row = lax.broadcasted_iota(jnp.int32, (n, LANES), 0)
    near = row // outer
    step = jnp.zeros_like(row)
    for k, t in enumerate(order(inner), 1):
        step = jnp.where(near == k, t, step)
    token = partner(me // inner, row % outer, outer) * inner + partner(me % inner, step, inner)
    slots = bites.shape[0] * bites.shape[1]
    count = jnp.zeros((n, LANES), jnp.float32)
    for b in range(bites.shape[0]):
        for c in range(bites.shape[1] // LANES):
            count += (bites[b : b + 1, c * LANES : (c + 1) * LANES] == token).astype(jnp.float32)
    total = jnp.sum(count, axis=1, keepdims=True)
    weight[...] = jnp.broadcast_to(total * (1.0 / (width * slots**0.5)), (n, LANES))


def split_rows(train, hi, lo):
    @pl.loop(0, train.shape[0] // 16)
    def _(r):
        span = pl.ds(pl.multiple_of(r * 16, 16), 16)
        hi[span], lo[span] = halves(train[span])


def split_kernel(outer, inner, width, act, grad, bites, after, a_hi, a_lo, g_hi, g_lo, weight, index, sem):
    copy = pltpu.make_async_copy(bites, index, sem)
    copy.start()
    split_rows(act, a_hi, a_lo)
    split_rows(grad, g_hi, g_lo)
    copy.wait()
    weigh(outer, inner, width, index, weight)


def split(outer, inner, width, act, grad, bites, after):
    half = pltpu.VMEM(act.shape, jnp.bfloat16)
    return pl.pallas_call(
        functools.partial(split_kernel, outer, inner, width),
        out_shape=[half] * 4 + [pltpu.VMEM((outer * inner, LANES), jnp.float32)],
        in_specs=[WHOLE, WHOLE, ANYWHERE, ANYWHERE],
        out_specs=[WHOLE] * 5,
        scratch_shapes=[pltpu.VMEM(bites.shape, jnp.int32), pltpu.SemaphoreType.DMA],
        compiler_params=SMALL,
        name="split",
    )(*vmem(act, grad), pltpu.with_memory_space_constraint(bites, pltpu.HBM), *vmem(after))


def rows_of(pool, which, n, cols, block):
    tops, bottoms = [], []
    for q in range(cols // LANES):
        top, bottom = halves(pool[pl.ds(which * (block // 2) + q, n, stride=block)])
        tops.append(top)
        bottoms.append(bottom)
    return jnp.concatenate([jnp.concatenate(tops, axis=1), jnp.concatenate(bottoms, axis=1)], axis=0)


def product(both, hi, lo, start, rows):
    n = both.shape[0] // 2
    dims = (((1,), (1,)), ((), ()))
    span = pl.ds(pl.multiple_of(start, 32), rows)
    one = lax.dot_general(both, hi[span], dims, preferred_element_type=jnp.float32)
    two = lax.dot_general(both[:n], lo[span], dims, preferred_element_type=jnp.float32)
    return one[:n] + one[n:] + two


def device_grams(act_pool, grad_pool, parts, weight, to, share):
    a_hi, a_lo, g_hi, g_lo = parts
    act = product(act_pool[...], a_hi, a_lo, to * share, share) * weight[:, :share]
    grad = product(grad_pool[...], g_hi, g_lo, to * share, share)
    return jnp.concatenate([act, grad], axis=1)


def chip_grams(act_pool, grad_pool, parts, weight, chip, share):
    a_hi, a_lo, g_hi, g_lo = parts
    rows = CORES * share
    act = product(act_pool[...], a_hi, a_lo, chip * rows, rows) * weight[:, :rows]
    grad = product(grad_pool[...], g_hi, g_lo, chip * rows, rows)
    return [
        jnp.concatenate([act[:, c * share : (c + 1) * share], grad[:, c * share : (c + 1) * share]], axis=1)
        for c in range(CORES)
    ]


def swap(pieces, me, mine, other):
    mine[...] = jnp.where(me % CORES == 0, pieces[0], pieces[1])
    other[...] = jnp.where(me % CORES == 0, pieces[1], pieces[0])


def far_kernel(outer, inner, feat, a_hi, a_lo, g_hi, g_lo, weight, *refs):
    pieces, (act_pool, grad_pool, *outs), (pool,) = refs[: inner + 1], refs[inner + 1 : -1], refs[-1:]
    n = outer * inner
    rows, cols = a_hi.shape
    block = pieces[0].shape[0] // outer
    start = 0
    for piece in pieces:
        pool[pl.ds(start, piece.shape[0])] = piece[...]
        start += piece.shape[0]
    act_pool[...] = rows_of(pool, 0, n, cols, block)
    grad_pool[...] = rows_of(pool, 1, n, cols, block)
    me = lax.axis_index("feat")
    chips = feat // CORES
    for s in range(1, chips):
        to = partner_to(me // CORES, s, chips)
        got = chip_grams(act_pool, grad_pool, (a_hi, a_lo, g_hi, g_lo), weight, to, rows // feat)
        swap(got, me, outs[CORES * (s - 1)], outs[CORES * (s - 1) + 1])


def near_kernel(feat, step, a_hi, a_lo, g_hi, g_lo, weight, act_pool, grad_pool, after, out):
    me = lax.axis_index("feat")
    to = me // CORES * CORES + (me + step) % CORES
    out[...] = device_grams(act_pool, grad_pool, (a_hi, a_lo, g_hi, g_lo), weight, to, a_hi.shape[0] // feat)


def far(outer, inner, feat, parts, pieces):
    n = outer * inner
    rows, cols = parts[0].shape
    args = vmem(*parts, *pieces)
    piece = pltpu.VMEM((n, 2 * rows // feat), jnp.float32)
    outs = [pltpu.VMEM((2 * n, cols), jnp.bfloat16)] * 2 + [piece] * (feat - CORES)
    return pl.pallas_call(
        functools.partial(far_kernel, outer, inner, feat),
        out_shape=outs,
        in_specs=[WHOLE] * len(args),
        out_specs=[WHOLE] * len(outs),
        scratch_shapes=[pltpu.VMEM((inner * pieces[0].shape[0], LANES), jnp.float32)],
        compiler_params=pltpu.CompilerParams(vmem_limit_bytes=8 << 20),
        name="far",
    )(*args)


def near(feat, step, parts, pools, after):
    args = vmem(*parts, *pools, after)
    return pl.pallas_call(
        functools.partial(near_kernel, feat, step),
        out_shape=pltpu.VMEM((pools[0].shape[0] // 2, 2 * parts[0].shape[0] // feat), jnp.float32),
        in_specs=[WHOLE] * (len(args) - 1) + [ANYWHERE],
        out_specs=WHOLE,
        compiler_params=pltpu.CompilerParams(vmem_limit_bytes=8 << 20),
        name="near",
    )(*args)


def add_kernel(*refs):
    *parts, out = refs
    total = parts[0][...]
    for part in parts[1:]:
        total += part[...]
    out[...] = total


def tally(parts):
    return pl.pallas_call(
        add_kernel,
        out_shape=pltpu.VMEM(parts[0].shape, jnp.float32),
        in_specs=[WHOLE] * len(parts),
        out_specs=WHOLE,
        compiler_params=SMALL,
        name="add",
    )(*vmem(*parts))


def finish_kernel(*refs):
    *parts, out = refs
    total = parts[0][...]
    for part in parts[1:]:
        total += part[...]
    share = out.shape[1]
    out[...] = jnp.sum(total[:, :share] * total[:, share:], axis=0, keepdims=True)


def body(train_act, train_grad, pool_act, pool_grad, bites):
    tok, feat = lax.axis_size("tok"), lax.axis_size("feat")
    rows, cols = train_act.shape
    outer, inner = factors(tok)
    own = prepare(pool_act.reshape(-1, LANES), pool_grad.reshape(-1, LANES))

    own = stage(own, train_act, train_grad)
    *direct, apart = order(inner)

    def exchange(value, s, t):
        at = [partner(i // inner, s, outer) * inner + partner(i % inner, t, inner) for i in range(tok)]
        return lax.ppermute(value, "tok", [(source, i) for i, source in enumerate(at)])

    across = [exchange(own, s, 0) for s in range(1, outer)]
    early = exchange(own, 0, apart)
    held = join([own, *across])
    late = join(across, early)
    pieces = [held] + [exchange(held, 0, t) for t in direct] + [early, exchange(late, 0, apart)]
    parts = split(outer, inner, cols * feat, train_act, train_grad, bites, held)
    act_pool, grad_pool, *sends = far(outer, inner, feat, parts, pieces)
    chips = feat // CORES
    got = []
    for s, send in enumerate(sends, CORES):
        pairs = [(i, partner_to(i // CORES, s // CORES, chips) * CORES + (i + s) % CORES) for i in range(feat)]
        got.append(lax.ppermute(send, "feat", pairs))
    other = near(feat, 1, parts, (act_pool, grad_pool), sends[0])
    beside = lax.ppermute(other, "feat", [(i, i // CORES * CORES + (i + 1) % CORES) for i in range(feat)])
    got = [tally([*got, near(feat, 0, parts, (act_pool, grad_pool), other)]), beside]
    score = pl.pallas_call(
        finish_kernel,
        out_shape=jax.ShapeDtypeStruct((1, rows // feat), jnp.float32),
        in_specs=[WHOLE] * len(got),
        out_specs=WHOLE,
        compiler_params=SMALL,
        name="finish",
    )(*vmem(*got))
    return score.reshape(-1)


def solution(mesh):
    return jax.shard_map(
        body,
        mesh=mesh,
        in_specs=(P("tok", "feat"), P("tok", "feat"), P("tok", "feat"), P("tok", "feat"), P()),
        out_specs=P(("tok", "feat")),
        check_vma=False,
    )
```

```python
import functools

import jax
import jax.numpy as jnp
from jax import lax
from jax.experimental import pallas as pl
from jax.experimental.pallas import tpu as pltpu
from jax.sharding import PartitionSpec as P

LANES = 128
CORES = 2


def halves(x):
    hi = x.astype(jnp.bfloat16)
    lo = (x - hi.astype(jnp.float32)).astype(jnp.bfloat16)
    return hi, lo


def partner(index, step, size):
    if size & (size - 1) == 0:
        return index ^ step
    return (index + size - step) % size


def partner_to(index, step, size):
    if size & (size - 1) == 0:
        return index ^ step
    return (index + step) % size


def factors(n):
    outer = max(d for d in range(1, n + 1) if n % d == 0 and d * d <= n)
    return outer, n // outer


def order(inner):
    apart = inner // 2
    return [t for t in range(1, inner) if t != apart] + [apart]


def vmem(*xs):
    return [pltpu.with_memory_space_constraint(x, pltpu.VMEM) for x in xs]


WHOLE = pl.BlockSpec(memory_space=pltpu.VMEM)
SMALL = pltpu.CompilerParams(vmem_limit_bytes=2 << 20)
ANYWHERE = pl.BlockSpec(memory_space=pl.ANY)


def prepare_kernel(act, grad, own, sems):
    block = act.shape[0]
    copies = [pltpu.make_async_copy(src, own.at[pl.ds(i * block, block)], sems.at[i]) for i, src in enumerate((act, grad))]
    for copy in copies:
        copy.start()
    for copy in copies:
        copy.wait()


def prepare(act, grad):
    return pl.pallas_call(
        prepare_kernel,
        out_shape=pltpu.VMEM((2 * act.shape[0], LANES), jnp.float32),
        in_specs=[ANYWHERE, ANYWHERE],
        out_specs=WHOLE,
        scratch_shapes=[pltpu.SemaphoreType.DMA((2,))],
        compiler_params=SMALL,
        name="prepare",
    )(pltpu.with_memory_space_constraint(act, pltpu.HBM), pltpu.with_memory_space_constraint(grad, pltpu.HBM))


def stage_kernel(own, train_act, train_grad, out):
    out[...] = own[...]


def stage(own, *trains):
    return pl.pallas_call(
        stage_kernel,
        out_shape=pltpu.VMEM(own.shape, jnp.float32),
        in_specs=[WHOLE, ANYWHERE, ANYWHERE],
        out_specs=WHOLE,
        compiler_params=SMALL,
        name="stage",
    )(*vmem(own), *[pltpu.with_memory_space_constraint(x, pltpu.HBM) for x in trains])


def join_kernel(count, *refs):
    out = refs[-1]
    block = refs[0].shape[0]
    for i, part in enumerate(refs[:count]):
        out[pl.ds(i * block, block)] = part[...]


def join(parts, *after):
    block = parts[0].shape[0]
    return pl.pallas_call(
        functools.partial(join_kernel, len(parts)),
        out_shape=pltpu.VMEM((len(parts) * block, LANES), jnp.float32),
        in_specs=[WHOLE] * len(parts) + [ANYWHERE] * len(after),
        out_specs=WHOLE,
        compiler_params=SMALL,
        name="join",
    )(*vmem(*parts, *after))


def weigh(outer, inner, width, bites, weight):
    n = outer * inner
    me = lax.axis_index("tok")
    row = lax.broadcasted_iota(jnp.int32, (n, LANES), 0)
    near = row // outer
    step = jnp.zeros_like(row)
    for k, t in enumerate(order(inner), 1):
        step = jnp.where(near == k, t, step)
    token = partner(me // inner, row % outer, outer) * inner + partner(me % inner, step, inner)
    slots = bites.shape[0] * bites.shape[1]
    count = jnp.zeros((n, LANES), jnp.float32)
    for b in range(bites.shape[0]):
        for c in range(bites.shape[1] // LANES):
            count += (bites[b : b + 1, c * LANES : (c + 1) * LANES] == token).astype(jnp.float32)
    total = jnp.sum(count, axis=1, keepdims=True)
    weight[...] = jnp.broadcast_to(total * (1.0 / (width * slots**0.5)), (n, LANES))


def split_rows(train, wide):
    cols = train.shape[1]

    @pl.loop(0, train.shape[0] // 16)
    def _(r):
        span = pl.ds(pl.multiple_of(r * 16, 16), 16)
        wide[span, :cols], wide[span, cols:] = halves(train[span])


def split_kernel(outer, inner, width, act, grad, bites, after, act_wide, grad_wide, weight, index, sem):
    copy = pltpu.make_async_copy(bites, index, sem)
    copy.start()
    split_rows(act, act_wide)
    split_rows(grad, grad_wide)
    copy.wait()
    weigh(outer, inner, width, index, weight)


def split(outer, inner, width, act, grad, bites, after):
    wide = pltpu.VMEM((act.shape[0], 2 * act.shape[1]), jnp.bfloat16)
    return pl.pallas_call(
        functools.partial(split_kernel, outer, inner, width),
        out_shape=[wide] * 2 + [pltpu.VMEM((outer * inner, LANES), jnp.float32)],
        in_specs=[WHOLE, WHOLE, ANYWHERE, ANYWHERE],
        out_specs=[WHOLE] * 3,
        scratch_shapes=[pltpu.VMEM(bites.shape, jnp.int32), pltpu.SemaphoreType.DMA],
        compiler_params=SMALL,
        name="split",
    )(*vmem(act, grad), pltpu.with_memory_space_constraint(bites, pltpu.HBM), *vmem(after))


def rows_of(pool, which, n, cols, block):
    tops, bottoms = [], []
    for q in range(cols // LANES):
        top, bottom = halves(pool[pl.ds(which * (block // 2) + q, n, stride=block)])
        tops.append(top)
        bottoms.append(bottom)
    return jnp.concatenate([jnp.concatenate(tops, axis=1), jnp.concatenate(bottoms, axis=1)], axis=0)


def product(both, wide, start, rows):
    n = both.shape[0] // 2
    dims = (((1,), (1,)), ((), ()))
    span = pl.ds(pl.multiple_of(start, 32), rows)
    out = lax.dot_general(jnp.concatenate([both, both], axis=1), wide[span], dims, preferred_element_type=jnp.float32)
    return out[:n] + out[n:]


def device_grams(act_pool, grad_pool, parts, weight, to, share):
    act_wide, grad_wide = parts
    act = product(act_pool[...], act_wide, to * share, share) * weight[:, :share]
    grad = product(grad_pool[...], grad_wide, to * share, share)
    return jnp.concatenate([act, grad], axis=1)


def chip_grams(act_pool, grad_pool, parts, weight, chip, share):
    act_wide, grad_wide = parts
    rows = CORES * share
    act = product(act_pool[...], act_wide, chip * rows, rows) * weight[:, :rows]
    grad = product(grad_pool[...], grad_wide, chip * rows, rows)
    return [
        jnp.concatenate([act[:, c * share : (c + 1) * share], grad[:, c * share : (c + 1) * share]], axis=1)
        for c in range(CORES)
    ]


def swap(pieces, me, mine, other):
    mine[...] = jnp.where(me % CORES == 0, pieces[0], pieces[1])
    other[...] = jnp.where(me % CORES == 0, pieces[1], pieces[0])


def far_kernel(outer, inner, feat, act_wide, grad_wide, weight, *refs):
    pieces, (act_pool, grad_pool, *outs), (pool,) = refs[: inner + 1], refs[inner + 1 : -1], refs[-1:]
    n = outer * inner
    rows, cols = act_wide.shape[0], act_pool.shape[1]
    block = pieces[0].shape[0] // outer
    start = 0
    for piece in pieces:
        pool[pl.ds(start, piece.shape[0])] = piece[...]
        start += piece.shape[0]
    act_pool[...] = rows_of(pool, 0, n, cols, block)
    grad_pool[...] = rows_of(pool, 1, n, cols, block)
    me = lax.axis_index("feat")
    chips = feat // CORES
    for s in range(1, chips):
        to = partner_to(me // CORES, s, chips)
        got = chip_grams(act_pool, grad_pool, (act_wide, grad_wide), weight, to, rows // feat)
        swap(got, me, outs[CORES * (s - 1)], outs[CORES * (s - 1) + 1])


def near_kernel(feat, step, act_wide, grad_wide, weight, act_pool, grad_pool, after, out):
    me = lax.axis_index("feat")
    to = me // CORES * CORES + (me + step) % CORES
    out[...] = device_grams(act_pool, grad_pool, (act_wide, grad_wide), weight, to, act_wide.shape[0] // feat)


def far(outer, inner, feat, parts, pieces):
    n = outer * inner
    rows, cols = parts[0].shape[0], parts[0].shape[1] // 2
    args = vmem(*parts, *pieces)
    piece = pltpu.VMEM((n, 2 * rows // feat), jnp.float32)
    outs = [pltpu.VMEM((2 * n, cols), jnp.bfloat16)] * 2 + [piece] * (feat - CORES)
    return pl.pallas_call(
        functools.partial(far_kernel, outer, inner, feat),
        out_shape=outs,
        in_specs=[WHOLE] * len(args),
        out_specs=[WHOLE] * len(outs),
        scratch_shapes=[pltpu.VMEM((inner * pieces[0].shape[0], LANES), jnp.float32)],
        compiler_params=pltpu.CompilerParams(vmem_limit_bytes=8 << 20),
        name="far",
    )(*args)


def near(feat, step, parts, pools, after):
    args = vmem(*parts, *pools, after)
    return pl.pallas_call(
        functools.partial(near_kernel, feat, step),
        out_shape=pltpu.VMEM((pools[0].shape[0] // 2, 2 * parts[0].shape[0] // feat), jnp.float32),
        in_specs=[WHOLE] * (len(args) - 1) + [ANYWHERE],
        out_specs=WHOLE,
        compiler_params=pltpu.CompilerParams(vmem_limit_bytes=8 << 20),
        name="near",
    )(*args)


def add_kernel(*refs):
    *parts, out = refs
    total = parts[0][...]
    for part in parts[1:]:
        total += part[...]
    out[...] = total


def tally(parts):
    return pl.pallas_call(
        add_kernel,
        out_shape=pltpu.VMEM(parts[0].shape, jnp.float32),
        in_specs=[WHOLE] * len(parts),
        out_specs=WHOLE,
        compiler_params=SMALL,
        name="add",
    )(*vmem(*parts))


def finish_kernel(*refs):
    *parts, out = refs
    total = parts[0][...]
    for part in parts[1:]:
        total += part[...]
    share = out.shape[1]
    out[...] = jnp.sum(total[:, :share] * total[:, share:], axis=0, keepdims=True)


def body(train_act, train_grad, pool_act, pool_grad, bites):
    tok, feat = lax.axis_size("tok"), lax.axis_size("feat")
    rows, cols = train_act.shape
    outer, inner = factors(tok)
    own = prepare(pool_act.reshape(-1, LANES), pool_grad.reshape(-1, LANES))

    own = stage(own, train_act, train_grad)
    *direct, apart = order(inner)

    def exchange(value, s, t):
        at = [partner(i // inner, s, outer) * inner + partner(i % inner, t, inner) for i in range(tok)]
        return lax.ppermute(value, "tok", [(source, i) for i, source in enumerate(at)])

    across = [exchange(own, s, 0) for s in range(1, outer)]
    early = exchange(own, 0, apart)
    held = join([own, *across])
    late = join(across, early)
    pieces = [held] + [exchange(held, 0, t) for t in direct] + [early, exchange(late, 0, apart)]
    parts = split(outer, inner, cols * feat, train_act, train_grad, bites, held)
    act_pool, grad_pool, *sends = far(outer, inner, feat, parts, pieces)
    chips = feat // CORES
    got = []
    for s, send in enumerate(sends, CORES):
        pairs = [(i, partner_to(i // CORES, s // CORES, chips) * CORES + (i + s) % CORES) for i in range(feat)]
        got.append(lax.ppermute(send, "feat", pairs))
    other = near(feat, 1, parts, (act_pool, grad_pool), sends[0])
    beside = lax.ppermute(other, "feat", [(i, i // CORES * CORES + (i + 1) % CORES) for i in range(feat)])
    got = [tally([*got, near(feat, 0, parts, (act_pool, grad_pool), other)]), beside]
    score = pl.pallas_call(
        finish_kernel,
        out_shape=jax.ShapeDtypeStruct((1, rows // feat), jnp.float32),
        in_specs=[WHOLE] * len(got),
        out_specs=WHOLE,
        compiler_params=SMALL,
        name="finish",
    )(*vmem(*got))
    return score.reshape(-1)


def solution(mesh):
    return jax.shard_map(
        body,
        mesh=mesh,
        in_specs=(P("tok", "feat"), P("tok", "feat"), P("tok", "feat"), P("tok", "feat"), P()),
        out_specs=P(("tok", "feat")),
        check_vma=False,
    )
```
